32 devices in a mesh: expert: 8 (over y, x, core), dp: 4 (over z).
Axes of the slice: x: 2, y: 2, z: 4, core: 2. Of those that a mesh axis runs over, the one named last changes fastest.
Arguments:
- tokens: bfloat16 [4, 4096, 2048], P('dp', 'expert'), may hold values from -6 to 6
- cotangent: bfloat16 [4, 4096, 2048], P('dp', 'expert'), may hold values from -0.13183594 to 0.13183594
- routes: int32 [4, 4096, 1], P('dp', 'expert'), may hold values from 0 to 7; in each aligned block of 512 rows (0 to 511, 512 to 1023, ..., all dimensions but the last counted through in order) at most 128 rows name the same one
- owner: int32 [8], replicated, may hold values from 0 to 7, as said below
- master: float32 [8, 2048, 2304], P('expert', 'dp'), may hold values from -0.125 to 0.125
- moment1: float32 [8, 2048, 2304], P('expert', 'dp'), may hold values from -1.8 to 1.8
- moment2: float32 [8, 2048, 2304], P('expert', 'dp'), may hold values from 0.01 to 1
Outputs:
- token_grad: bfloat16 [4, 4096, 2048], P('dp', 'expert')
- new_master: float32 [8, 2048, 2304], P('expert', 'dp')
- new_moment1: float32 [8, 2048, 2304], P('expert', 'dp')
- new_moment2: float32 [8, 2048, 2304], P('expert', 'dp')
The draws below stay inside these ranges and needn't reach their ends.
Inputs may be any that keep to these rules, and one draw needn't show every extreme that they name: owner[j] is j or j xor (4), and owner[j] == j exactly when the same holds for j xor (4); at least one pair moves. `routes`: among the 512 tokens of one device at most 128 choose one expert, and some expert is chosen by exactly 128.
All inputs are finite; a program needn't handle non-finite values.
Results may differ from the reference program's by a relative error of at most 0.012.
Values may be sent and summed in bfloat16 or wider, within the bound.
A program may use at most 128 MiB of HBM per device.

```python
import math
import jax
import jax.numpy as jnp
import numpy as np
from jax import lax

D = 2048
HID = 768
TOK_DEV = 512
EXPERTS = 8
CAP = 128
N_EXPERT = 8
N_DP = 4


def draw_owner(key, part):
    key = jax.random.fold_in(key, 7)
    half = EXPERTS // 2
    flips = jax.random.randint(key, (half,), 0, 2)
    forced = jax.random.randint(jax.random.fold_in(key, 1), (), 0, half)
    flips = jnp.where(jnp.arange(half) == forced, 1, flips)
    index = jnp.arange(EXPERTS, dtype=jnp.int32)
    moved = flips[index % half]
    return jnp.where(moved == 1, jnp.bitwise_xor(index, half), index).astype(jnp.int32)


def level_of(key, extent, split, smallest, largest):
    def one(position, parts):
        heights = jax.random.uniform(jax.random.fold_in(jax.random.fold_in(key, 6), position), (parts,), jnp.float32, smallest / len(split), largest / len(split))
        return jnp.repeat(jnp.exp(heights), extent[position] // parts).reshape((-1,) + (1,) * (len(extent) - position - 1))

    loudness = one(*split[0])
    for cut in split[1:]:
        loudness = loudness * one(*cut)
    return loudness


def assign_block(stream_key, own, number, rows, amount, top, limit, skew):
    sequence = jax.random.permutation(stream_key, amount)
    heavy_load, usual = shares(amount, rows * top, limit, skew, True), shares(amount, rows * top, limit, skew, False)
    places = jnp.arange(amount)

    def named(tallies, offset_by):
        used = int((tallies > 0).sum())
        fixed = max(1, used // 4)
        moved = fixed + (places - fixed + offset_by * (used - fixed)) % max(1, amount - fixed)
        return jnp.zeros((amount,), jnp.int32).at[sequence[jnp.where(places < fixed, places, moved)]].set(jnp.asarray(tallies, jnp.int32))

    tallies = jnp.where(number % 4 == 0, named(heavy_load, number // 4), named(usual, number - number // 4 - 1))
    mixed = jax.random.permutation(jax.random.fold_in(own, 3), amount)
    donor, receiver = mixed[0:amount // 2 * 2:2], mixed[1:amount // 2 * 2:2]
    margin = jnp.minimum(tallies[donor] - 1, limit - tallies[receiver]) // 2
    margin = jnp.where((donor == sequence[0]) | (receiver == sequence[0]) | (tallies[receiver] == 0), 0, jnp.maximum(margin, 0))
    moved = jax.random.randint(jax.random.fold_in(own, 4), (amount // 2,), 0, 1 << 20) % (margin + 1)
    tallies = tallies.at[donor].add(-moved).at[receiver].add(moved)
    members = jnp.searchsorted(jnp.cumsum(tallies), jnp.arange(rows * top), side="right").astype(jnp.int32)
    grid = members.reshape(top, rows).T
    grid = grid[jax.random.permutation(jax.random.fold_in(own, 1), rows)]
    offset_by = jax.random.randint(jax.random.fold_in(own, 2), (rows, 1), 0, top)
    return jnp.take_along_axis(grid, (jnp.arange(top)[None, :] + offset_by) % top, axis=1)


def shares(number_of, total, limit, lean, full):
    loads = [(1 << 20) // math.isqrt(rank ** lean) + 1 for rank in range(1, number_of + 1)]
    largest = limit if full else min(limit, max(-(-total // number_of), total * loads[0] // sum(loads)))
    least = 1 if total - largest >= number_of - 1 else 0
    holding, surplus = [largest] + [least] * (number_of - 1), total - largest - least * (number_of - 1)
    while surplus > 0:
        free = [i for i in range(1, number_of) if holding[i] < largest] or [i for i in range(1, number_of) if holding[i] < limit]
        mass, left = sum([loads[i] for i in free]), surplus
        for i in free:
            extra = min(limit - holding[i], max(1, left * loads[i] // mass), surplus)
            holding[i] = holding[i] + extra
            surplus = surplus - extra
    return np.array(holding)


def noise(stream_key, extent, spread, limit, pieces=(), kind=jnp.bfloat16):
    drawn = spread * jax.random.normal(stream_key, extent, jnp.float32)
    if pieces:
        drawn = drawn * level_of(stream_key, extent, pieces, -0.22, 0.18)
    return jnp.clip(drawn, -limit, limit).astype(kind)


def setup_inputs(seed: int = 0) -> dict:
    seeds = jax.random.split(jax.random.key(seed), 8)
    tokens = noise(seeds[0], (N_DP, N_EXPERT * TOK_DEV, D), 1.0, 6.0, ((0, 4), (1, 8)))
    cotangent = noise(seeds[1], (N_DP, N_EXPERT * TOK_DEV, D), (1.0 / (TOK_DEV * N_DP) ** 0.5), 0.13183594, ((0, 4), (1, 8)))
    routes_keys = jax.random.split(jax.random.fold_in(seeds[2], 1), N_DP * (N_EXPERT * TOK_DEV) // TOK_DEV)
    routes_turns = jax.random.permutation(jax.random.fold_in(seeds[2], 3), N_DP * (N_EXPERT * TOK_DEV) // TOK_DEV)
    routes = jax.vmap(lambda own, number: assign_block(jax.random.fold_in(seeds[2], 2), own, number, TOK_DEV, N_EXPERT, 1, CAP, 2))(routes_keys, routes_turns).reshape((N_DP, N_EXPERT * TOK_DEV, 1))
    owner = draw_owner(jax.random.fold_in(seeds[7], 71), 0)
    master = noise(seeds[4], (EXPERTS, D, 3 * HID), D ** -0.5, 0.125, ((0, 8), (1, 4)), jnp.float32)
    moment1 = noise(seeds[5], (EXPERTS, D, 3 * HID), 0.3, 1.8, ((0, 8), (1, 4)), jnp.float32)
    moment2 = jnp.clip(jnp.exp(math.log(1.0) - 4.6051702 * jax.random.uniform(seeds[6], (EXPERTS, D, 3 * HID), jnp.float32) ** level_of(seeds[6], (EXPERTS, D, 3 * HID), ((0, 8), (1, 4)), -0.2, 0.2)), 0.01, 1.0)
    return {"tokens": tokens, "cotangent": cotangent, "routes": routes, "owner": owner, "master": master, "moment1": moment1, "moment2": moment2}


def reference(tokens, cotangent, routes, owner, master, moment1, moment2):
    half = EXPERTS // 2
    ids = jnp.arange(EXPERTS, dtype=jnp.int32)
    source = jnp.where(owner == ids, ids, jnp.bitwise_xor(ids, half)).astype(jnp.int32)
    placed_master = master[source]
    placed_first = moment1[source]
    placed_second = moment2[source]
    weights = placed_master.astype(jnp.bfloat16).astype(jnp.float32)
    gate_up = weights[:, :, :2 * HID]
    down = weights[:, :, 2 * HID:]

    def group(total, inputs):
        x_group, dy_group, route_group = inputs
        route_pos = route_group.reshape(EXPERTS, TOK_DEV)
        onehot = (route_pos[:, :, None] == ids[None, None, :]).astype(jnp.int32)
        slot = lax.optimization_barrier(jnp.sum((jnp.cumsum(onehot, axis=1) - 1) * onehot, axis=2))
        anchor = jnp.arange(EXPERTS, dtype=jnp.int32)[:, None]
        flat = (route_pos * (EXPERTS * CAP) + anchor * CAP + slot).reshape(-1).astype(jnp.int32)
        box_x = jnp.zeros((EXPERTS * EXPERTS * CAP, D), jnp.bfloat16).at[flat].set(x_group)
        box_dy = jnp.zeros((EXPERTS * EXPERTS * CAP, D), jnp.bfloat16).at[flat].set(dy_group)
        rows_x = box_x.reshape(EXPERTS, EXPERTS * CAP, D).astype(jnp.float32)
        rows_dy = box_dy.reshape(EXPERTS, EXPERTS * CAP, D).astype(jnp.float32)
        pre = jnp.einsum('erd,edk->erk', rows_x, gate_up)
        gate_pre = pre[:, :, :HID]
        up_pre = pre[:, :, HID:]
        sig = jax.nn.sigmoid(gate_pre)
        act = gate_pre * sig
        hidden = (act * up_pre).astype(jnp.bfloat16).astype(jnp.float32)
        d_hidden = jnp.einsum('erd,edk->erk', rows_dy, down)
        d_gate = (d_hidden * up_pre * sig * (1.0 + gate_pre * (1.0 - sig))).astype(jnp.bfloat16)
        d_up = (d_hidden * act).astype(jnp.bfloat16)
        d_both = jnp.concatenate([d_gate, d_up], axis=2).astype(jnp.float32)
        part_gu = jnp.einsum('erd,erk->edk', rows_x, d_both)
        part_down = jnp.einsum('erd,erk->edk', rows_dy, hidden)
        partial_value = jnp.concatenate([part_gu, part_down], axis=2).astype(jnp.bfloat16)
        in_grad = jnp.einsum('erk,edk->erd', d_both, gate_up).astype(jnp.bfloat16)
        token_rows = in_grad.reshape(EXPERTS * EXPERTS * CAP, D)[flat]
        return (total + partial_value.astype(jnp.float32), token_rows)
    start = jnp.zeros((EXPERTS, D, 3 * HID), jnp.float32)
    grad, token_grad = lax.scan(group, start, (tokens, cotangent, routes[:, :, 0]))
    new_first = 0.9 * placed_first + 0.1 * grad
    new_second = 0.95 * placed_second + 0.05 * grad * grad
    step = new_first / (1.0 - 0.9 ** 10) / (jnp.sqrt(new_second / (1.0 - 0.95 ** 10)) + 1e-08)
    new_master = placed_master - 0.003 * (step + 0.1 * placed_master)
    return (token_grad, new_master, new_first, new_second)
```

```python
import functools

import jax
import jax.numpy as jnp
from jax import lax
from jax.experimental import pallas as pl
from jax.experimental.pallas import tpu as pltpu
from jax.sharding import PartitionSpec as P

CHUNKS = 3
BF = jnp.bfloat16
F32 = jnp.float32


def swapped(value, apart):
    size = lax.axis_size("expert")
    return lax.ppermute(value, "expert", [(i, i ^ 1 << apart) for i in range(size)])


def pack_body(gate, up, down, out):
    width = gate.shape[1]
    out[:, :width] = gate[...].astype(BF)
    out[:, width : 2 * width] = up[...].astype(BF)
    out[:, 2 * width :] = down[...].astype(BF)


def pack(master, chunk):
    rows, columns = master.shape
    width = columns // (3 * CHUNKS)
    tile = min(rows, 128)
    return pl.pallas_call(
        pack_body,
        grid=(rows // tile,),
        in_specs=[
            pl.BlockSpec((tile, width), functools.partial(lambda c, i: (i, c), part * CHUNKS + chunk))
            for part in range(3)
        ],
        out_specs=pl.BlockSpec((tile, 3 * width), lambda i: (i, 0)),
        out_shape=jax.ShapeDtypeStruct((rows, 3 * width), BF),
        cost_estimate=pl.CostEstimate(flops=0, bytes_accessed=6 * rows * 3 * width, transcendentals=0),
    )(master, master, master)


def narrow_body(source, out):
    out[...] = source[...].astype(BF)


def narrow(state):
    rows, columns = state.shape
    tile = min(rows, 128)
    return pl.pallas_call(
        narrow_body,
        grid=(rows // tile,),
        in_specs=[pl.BlockSpec((tile, columns), lambda i: (i, 0))],
        out_specs=pl.BlockSpec((tile, columns), lambda i: (i, 0)),
        out_shape=jax.ShapeDtypeStruct((rows, columns), BF),
        cost_estimate=pl.CostEstimate(flops=0, bytes_accessed=6 * rows * columns, transcendentals=0),
    )(state)


def update_body(keep, master, first, second, other_master, other_first, other_second, grad, *rest):
    new_master, new_first, new_second = rest[-3:]
    stay = keep[0] == 1
    placed = jnp.where(stay, master[...], other_master[...].astype(F32))
    m1 = jnp.where(stay, first[...], other_first[...].astype(F32))
    m2 = jnp.where(stay, second[...], other_second[...].astype(F32))
    g = grad[...].astype(F32)
    m1 = 0.9 * m1 + 0.1 * g
    m2 = 0.95 * m2 + 0.05 * g * g
    step = m1 / (1.0 - 0.9**10) / (jnp.sqrt(m2 / (1.0 - 0.95**10)) + 1e-08)
    new_first[...] = m1
    new_second[...] = m2
    new_master[...] = placed - 0.003 * (step + 0.1 * placed)


def update(keep, states, others, grad, chunk, before):
    rows, columns = states[0].shape
    width = columns // (3 * CHUNKS)
    tile = min(rows, 256)
    wide = pl.BlockSpec((tile, width), lambda part, i: (i, part * CHUNKS + chunk))
    near = pl.BlockSpec((tile, width), lambda part, i: (i, part))
    count = 0 if before is None else 3
    return pl.pallas_call(
        update_body,
        grid=(3, rows // tile),
        in_specs=[pl.BlockSpec(memory_space=pltpu.SMEM)]
        + [wide] * 3
        + [near, wide, wide, near]
        + [pl.BlockSpec(memory_space=pl.ANY)] * count,
        out_specs=[wide] * 3,
        out_shape=[jax.ShapeDtypeStruct((rows, columns), F32)] * 3,
        input_output_aliases={8 + i: i for i in range(count)},
        cost_estimate=pl.CostEstimate(
            flops=20 * rows * 3 * width, bytes_accessed=32 * rows * 3 * width, transcendentals=0
        ),
    )(keep, *states, *others, grad, *(before or ()))


def after(value, *earlier):
    return lax.optimization_barrier((value, *earlier))[0]


def per_device(tokens, cotangent, routes, owner, master, moment1, moment2):
    experts = lax.axis_size("expert")
    bit = experts.bit_length() - 2
    position = lax.axis_index("expert")
    keep = owner[position] == position
    flag = keep.astype(jnp.int32).reshape(1)
    states = (master[0], moment1[0], moment2[0])
    width = master.shape[2] // (3 * CHUNKS)
    tok_count = tokens.shape[1]
    capacity = 2 * tok_count // experts
    slots = experts * capacity
    features = tokens.shape[2]

    packed = [pack(states[0], c) for c in range(CHUNKS)]
    route_ids = routes[0, :, 0]
    columns = jnp.arange(experts, dtype=jnp.int32)
    onehot = (route_ids[:, None] == columns[None, :]).astype(jnp.int32)
    slot = jnp.sum((jnp.cumsum(onehot, axis=0) - 1) * onehot, axis=1)
    flat = route_ids * capacity + slot
    place = (jnp.arange(slots, dtype=jnp.int32)[:, None] == flat[None, :]).astype(BF)
    take = (flat[:, None] == jnp.arange(slots, dtype=jnp.int32)[None, :]).astype(BF)

    def exchange(rows):
        return lax.all_to_all(
            rows.reshape(experts, capacity, features), "expert", split_axis=0, concat_axis=0, tiled=True
        ).reshape(slots, features)

    send_x = jnp.dot(place, tokens[0], preferred_element_type=F32).astype(BF)
    send_dy = jnp.dot(place, cotangent[0], preferred_element_type=F32).astype(BF)

    def gathered(chunk, partner):
        placed = jnp.where(keep, packed[chunk], partner)
        return lax.all_gather(placed, "dp", axis=0, tiled=True)

    other = [None] * CHUNKS
    weights = [None] * CHUNKS
    other[0] = swapped(packed[0], bit)
    weights[0] = gathered(0, other[0])
    rows_x = exchange(after(send_x, other[0]))
    other[1] = swapped(after(packed[1], other[0]), bit)
    weights[1] = gathered(1, other[1])
    rows_dy = exchange(after(send_dy, rows_x))
    other[2] = swapped(after(packed[2], rows_x), bit)
    weights[2] = gathered(2, other[2])
    narrow_first = narrow(states[1])
    narrow_second = narrow(states[2])
    other_first = swapped(after(narrow_first, rows_dy), bit)
    other_second = swapped(after(narrow_second, other_first), bit)

    total = None
    grads = []
    for c in range(CHUNKS):
        gate_up = weights[c][:, : 2 * width]
        down = weights[c][:, 2 * width :]
        pre = jnp.dot(rows_x, gate_up, preferred_element_type=F32)
        gate_pre = pre[:, :width]
        up_pre = pre[:, width:]
        sig = jax.nn.sigmoid(gate_pre)
        act = gate_pre * sig
        hidden = (act * up_pre).astype(BF)
        d_hidden = jnp.dot(rows_dy, down, preferred_element_type=F32)
        d_gate = (d_hidden * up_pre * sig * (1.0 + gate_pre * (1.0 - sig))).astype(BF)
        d_up = (d_hidden * act).astype(BF)
        d_both = jnp.concatenate([d_gate, d_up], axis=1)
        left = jnp.einsum("rd,rk->dk", rows_x, d_both, preferred_element_type=F32)
        right = jnp.einsum("rd,rk->dk", rows_dy, hidden, preferred_element_type=F32)
        grads.append(
            lax.psum_scatter(
                jnp.concatenate([left.astype(BF), right.astype(BF)], axis=1),
                "dp",
                scatter_dimension=0,
                tiled=True,
            )
        )
        part = jnp.einsum("rk,dk->rd", d_both, gate_up, preferred_element_type=F32)
        total = part if total is None else total + part
    returned = exchange(total.astype(BF))
    token_grad = jnp.dot(take, returned, preferred_element_type=F32).astype(BF)

    made = None
    for c in range(CHUNKS):
        made = update(flag, states, (other[c], other_first, other_second), grads[c], c, made)
    return (token_grad[None], made[0][None], made[1][None], made[2][None])


def solution(mesh):
    placed = (
        P("dp", "expert", None),
        P("dp", "expert", None),
        P("dp", "expert", None),
        P(),
        P("expert", "dp", None),
        P("expert", "dp", None),
        P("expert", "dp", None),
    )
    return jax.shard_map(
        per_device,
        mesh=mesh,
        in_specs=placed,
        out_specs=(
            P("dp", "expert", None),
            P("expert", "dp", None),
            P("expert", "dp", None),
            P("expert", "dp", None),
        ),
        check_vma=False,
    )
```

```python
import functools

import jax
import jax.numpy as jnp
from jax import lax
from jax.experimental import pallas as pl
from jax.experimental.pallas import tpu as pltpu
from jax.sharding import PartitionSpec as P

CHUNKS = 3
BF = jnp.bfloat16
F32 = jnp.float32


def swapped(value, apart):
    size = lax.axis_size("expert")
    return lax.ppermute(value, "expert", [(i, i ^ 1 << apart) for i in range(size)])


def pack_body(gate, up, down, out):
    width = gate.shape[1]
    out[:, :width] = gate[...].astype(BF)
    out[:, width : 2 * width] = up[...].astype(BF)
    out[:, 2 * width :] = down[...].astype(BF)


def pack(master, chunk):
    rows, columns = master.shape
    width = columns // (3 * CHUNKS)
    tile = min(rows, 128)
    return pl.pallas_call(
        pack_body,
        grid=(rows // tile,),
        in_specs=[
            pl.BlockSpec((tile, width), functools.partial(lambda c, i: (i, c), part * CHUNKS + chunk))
            for part in range(3)
        ],
        out_specs=pl.BlockSpec((tile, 3 * width), lambda i: (i, 0)),
        out_shape=jax.ShapeDtypeStruct((rows, 3 * width), BF),
        cost_estimate=pl.CostEstimate(flops=0, bytes_accessed=6 * rows * 3 * width, transcendentals=0),
    )(master, master, master)


def narrow_body(source, out):
    out[...] = source[...].astype(BF)


def narrow(state):
    rows, columns = state.shape
    tile = min(rows, 128)
    return pl.pallas_call(
        narrow_body,
        grid=(rows // tile,),
        in_specs=[pl.BlockSpec((tile, columns), lambda i: (i, 0))],
        out_specs=pl.BlockSpec((tile, columns), lambda i: (i, 0)),
        out_shape=jax.ShapeDtypeStruct((rows, columns), BF),
        cost_estimate=pl.CostEstimate(flops=0, bytes_accessed=6 * rows * columns, transcendentals=0),
    )(state)


def update_body(keep, master, first, second, other_master, other_first, other_second, grad, *rest):
    new_master, new_first, new_second = rest[-3:]
    stay = keep[0] == 1
    placed = jnp.where(stay, master[...], other_master[...].astype(F32))
    m1 = jnp.where(stay, first[...], other_first[...].astype(F32))
    m2 = jnp.where(stay, second[...], other_second[...].astype(F32))
    g = grad[...].astype(F32)
    m1 = 0.9 * m1 + 0.1 * g
    m2 = 0.95 * m2 + 0.05 * g * g
    step = m1 / (1.0 - 0.9**10) / (jnp.sqrt(m2 / (1.0 - 0.95**10)) + 1e-08)
    new_first[...] = m1
    new_second[...] = m2
    new_master[...] = placed - 0.003 * (step + 0.1 * placed)


def update(keep, states, others, grad, chunk, before):
    rows, columns = states[0].shape
    width = columns // (3 * CHUNKS)
    tile = min(rows, 256)
    wide = pl.BlockSpec((tile, width), lambda part, i: (i, part * CHUNKS + chunk))
    near = pl.BlockSpec((tile, width), lambda part, i: (i, part))
    count = 0 if before is None else 3
    return pl.pallas_call(
        update_body,
        grid=(3, rows // tile),
        in_specs=[pl.BlockSpec(memory_space=pltpu.SMEM)]
        + [wide] * 3
        + [near, wide, wide, near]
        + [pl.BlockSpec(memory_space=pl.ANY)] * count,
        out_specs=[wide] * 3,
        out_shape=[jax.ShapeDtypeStruct((rows, columns), F32)] * 3,
        input_output_aliases={8 + i: i for i in range(count)},
        cost_estimate=pl.CostEstimate(
            flops=20 * rows * 3 * width, bytes_accessed=32 * rows * 3 * width, transcendentals=0
        ),
    )(keep, *states, *others, grad, *(before or ()))


def line_sum(partial):
    size = lax.axis_size("dp")
    place = lax.axis_index("dp")
    rows = partial.shape[0] // size

    def block(owner):
        return lax.dynamic_slice_in_dim(partial, jnp.clip(owner, 0, size - 1) * rows, rows, 0).astype(F32)

    up = down = jnp.zeros((), F32)
    for step in range(size - 1):
        lag = size - 1 - step
        up_sent = (block(place + lag) + up).astype(BF)
        down_sent = (block(place - lag) + down).astype(BF)
        up = lax.ppermute(up_sent, "dp", [(i, i + 1) for i in range(step + 1)]).astype(F32)
        down = lax.ppermute(
            down_sent, "dp", [(size - 1 - i, size - 2 - i) for i in range(step + 1)]
        ).astype(F32)
    return block(place) + up + down


def after(value, *earlier):
    return lax.optimization_barrier((value, *earlier))[0]


def per_device(tokens, cotangent, routes, owner, master, moment1, moment2):
    experts = lax.axis_size("expert")
    bit = experts.bit_length() - 2
    position = lax.axis_index("expert")
    keep = owner[position] == position
    flag = keep.astype(jnp.int32).reshape(1)
    states = (master[0], moment1[0], moment2[0])
    width = master.shape[2] // (3 * CHUNKS)
    tok_count = tokens.shape[1]
    capacity = 2 * tok_count // experts
    slots = experts * capacity
    features = tokens.shape[2]

    packed = [pack(states[0], c) for c in range(CHUNKS)]
    route_ids = routes[0, :, 0]
    columns = jnp.arange(experts, dtype=jnp.int32)
    onehot = (route_ids[:, None] == columns[None, :]).astype(jnp.int32)
    slot = jnp.sum((jnp.cumsum(onehot, axis=0) - 1) * onehot, axis=1)
    flat = route_ids * capacity + slot
    place = (jnp.arange(slots, dtype=jnp.int32)[:, None] == flat[None, :]).astype(BF)
    take = (flat[:, None] == jnp.arange(slots, dtype=jnp.int32)[None, :]).astype(BF)

    def exchange(rows):
        return lax.all_to_all(
            rows.reshape(experts, capacity, features), "expert", split_axis=0, concat_axis=0, tiled=True
        ).reshape(slots, features)

    send_x = jnp.dot(place, tokens[0], preferred_element_type=F32).astype(BF)
    send_dy = jnp.dot(place, cotangent[0], preferred_element_type=F32).astype(BF)

    def gathered(chunk, partner):
        placed = jnp.where(keep, packed[chunk], partner)
        return lax.all_gather(placed, "dp", axis=0, tiled=True)

    other = [None] * CHUNKS
    weights = [None] * CHUNKS
    other[0] = swapped(packed[0], bit)
    weights[0] = gathered(0, other[0])
    rows_x = exchange(after(send_x, other[0]))
    other[1] = swapped(after(packed[1], other[0]), bit)
    weights[1] = gathered(1, other[1])
    narrow_first = narrow(states[1])
    narrow_second = narrow(states[2])
    rows_dy = exchange(after(send_dy, rows_x, narrow_first, narrow_second))
    other[2] = swapped(after(packed[2], rows_x), bit)
    weights[2] = gathered(2, other[2])
    other_first = swapped(after(narrow_first, rows_dy), bit)
    other_second = swapped(after(narrow_second, other_first), bit)

    total = None
    grads = []
    for c in range(CHUNKS):
        if c == CHUNKS - 1:
            rows_x = after(rows_x, other_first)
        gate_up = weights[c][:, : 2 * width]
        down = weights[c][:, 2 * width :]
        pre = jnp.dot(rows_x, gate_up, preferred_element_type=F32)
        gate_pre = pre[:, :width]
        up_pre = pre[:, width:]
        sig = jax.nn.sigmoid(gate_pre)
        act = gate_pre * sig
        hidden = (act * up_pre).astype(BF)
        d_hidden = jnp.dot(rows_dy, down, preferred_element_type=F32)
        d_gate = (d_hidden * up_pre * sig * (1.0 + gate_pre * (1.0 - sig))).astype(BF)
        d_up = (d_hidden * act).astype(BF)
        d_both = jnp.concatenate([d_gate, d_up], axis=1)
        left = jnp.einsum("rd,rk->dk", rows_x, d_both, preferred_element_type=F32)
        right = jnp.einsum("rd,rk->dk", rows_dy, hidden, preferred_element_type=F32)
        partial = jnp.concatenate([left.astype(BF), right.astype(BF)], axis=1)
        if c % 2 == 1:
            grads.append(lax.psum_scatter(partial, "dp", scatter_dimension=0, tiled=True))
        else:
            grads.append(line_sum(partial))
        part = jnp.einsum("rk,dk->rd", d_both, gate_up, preferred_element_type=F32)
        total = part if total is None else total + part
    returned = exchange(total.astype(BF))
    token_grad = jnp.dot(take, after(returned, grads[-1]), preferred_element_type=F32).astype(BF)

    made = None
    for c in range(CHUNKS):
        made = update(flag, states, (other[c], other_first, other_second), grads[c], c, made)
    return (token_grad[None], made[0][None], made[1][None], made[2][None])


def solution(mesh):
    placed = (
        P("dp", "expert", None),
        P("dp", "expert", None),
        P("dp", "expert", None),
        P(),
        P("expert", "dp", None),
        P("expert", "dp", None),
        P("expert", "dp", None),
    )
    return jax.shard_map(
        per_device,
        mesh=mesh,
        in_specs=placed,
        out_specs=(
            P("dp", "expert", None),
            P("expert", "dp", None),
            P("expert", "dp", None),
            P("expert", "dp", None),
        ),
        check_vma=False,
    )
```
